256 devices in a mesh: blk: 16 (over z, y_lo), rep: 16 (over y_hi, x, core).
Axes of the slice: x: 4, y: 4 (y_hi: 2, y_lo: 2; y = y_hi * 2 + y_lo), z: 8, core: 2. Of those that a mesh axis runs over, the one named last changes fastest.
Arguments:
- features: bfloat16 [65536, 256], P(('blk', 'rep')), may hold values from -6 to 6
- w_self: bfloat16 [256, 256], replicated, may hold values from -0.375 to 0.375
- w_neigh: bfloat16 [256, 256], replicated, may hold values from -0.375 to 0.375
- bias: float32 [256], replicated, may hold values from -3 to 3
- cotangent: bfloat16 [65536, 256], P(('blk', 'rep')), may hold values from -6 to 6
- tile_values: bfloat16 [16, 16, 16, 12, 128, 128], P('blk', 'rep')
- tile_rows: int32 [16, 16, 16, 12], P('blk', 'rep'), may hold values from 0 to 31, as said below
- tile_cols: int32 [16, 16, 16, 12], P('blk', 'rep'), may hold values from 0 to 1
- tile_counts: int32 [16, 16, 16], P('blk', 'rep'), may hold values from 1 to 12, as said below
Outputs:
- output: bfloat16 [65536, 256], P(('blk', 'rep'))
- grad_features: bfloat16 [65536, 256], P(('blk', 'rep'))
- grad_self: float32 [256, 256], replicated
- grad_neigh: float32 [256, 256], replicated
- grad_bias: float32 [256], replicated
The draws below stay inside these ranges and needn't reach their ends.
Inputs may be any that keep to these rules, and one draw needn't show every extreme that they name: Among the live slots s < tile_counts[b, r, c] of one b, r, c, the pairs (tile_rows, tile_cols) are distinct; slots from tile_counts[b, r, c] on are not part of the adjacency. `tile_counts`: some entry equals 12 in every draw.
All inputs are finite; a program needn't handle non-finite values.
Results may differ from the reference program's by a relative error of at most 0.02.
Values may be sent and summed in bfloat16 or wider, within the bound.
No kernel may reach another device: no remote copies, remote signals or barrier semaphores. Data moves between devices by JAX's collectives and lax.ppermute only.
A program may use at most 64 MiB of HBM per device.

```python
import jax
import jax.numpy as jnp
from jax import lax

F = 256
TILE = 128
SLOTS = 12
ROWT = 2
NODES = 65536
N_BLK = 16
N_REP = 16


def tile_positions(key):
    places = N_REP * ROWT * ROWT
    scores = jax.random.randint(key, (N_BLK, N_REP, N_BLK, places), 0, 1 << 20) * places
    scores = scores + jnp.arange(places, dtype=jnp.int32)
    order = jnp.argsort(scores, axis=-1, stable=True)
    return order[..., :SLOTS].astype(jnp.int32)


def draw_tile_rows(key, part):
    chosen = tile_positions(key)
    return (chosen // ROWT).astype(jnp.int32)


def draw_tile_cols(key, part):
    chosen = tile_positions(key)
    return (chosen % ROWT).astype(jnp.int32)


def draw_tile_counts(key, part):
    key = jax.random.fold_in(key, 23)
    first, second, third = jax.random.split(key, 3)
    level = jax.random.randint(first, (N_BLK, 1, 1), (SLOTS + 2) // 3, SLOTS + 1)
    raw = jax.random.randint(second, (N_BLK, N_REP, N_BLK), 1, SLOTS + 1)
    counts = jnp.maximum(1, raw * level // SLOTS)
    spot = jax.random.randint(third, (), 0, N_BLK * N_REP * N_BLK)
    flat = jnp.arange(N_BLK * N_REP * N_BLK, dtype=jnp.int32).reshape(N_BLK, N_REP, N_BLK)
    return jnp.where(flat == spot, SLOTS, counts).astype(jnp.int32)


def draw_tile_values(key, part):
    key = jax.random.fold_in(key, 37)
    first, second = jax.random.split(key)
    shape = (N_BLK, N_REP, N_BLK, SLOTS, TILE, TILE)
    spread = (N_BLK * SLOTS * TILE / (24.0 * ROWT)) ** (-0.5)
    keep = jax.random.randint(second, shape, 0, 16) == 0
    values = jnp.clip(jax.random.normal(first, shape, jnp.float32), -6.0, 6.0)
    return jnp.where(keep, values * spread, 0.0).astype(jnp.bfloat16)


def block_scale(stream_key, extent, shards, least, top_value):
    gain = 1.0
    for axis_at, blocks in shards:
        draws = jax.random.uniform(jax.random.fold_in(jax.random.fold_in(stream_key, 6), axis_at), (blocks,), jnp.float32, least / len(shards), top_value / len(shards))
        gain = gain * jnp.repeat(jnp.exp(draws), extent[axis_at] // blocks).reshape((-1,) + (1,) * (len(extent) - 1 - axis_at))
    return gain


def noise(stream_key, dims, scale, reach, pieces=(), held_as=jnp.bfloat16):
    entries = scale * jax.random.normal(stream_key, dims, jnp.float32)
    if pieces:
        entries = entries * block_scale(stream_key, dims, pieces, -0.22, 0.18)
    return jnp.clip(entries, -reach, reach).astype(held_as)


def setup_inputs(seed: int = 0) -> dict:
    key_list = jax.random.split(jax.random.key(seed), 10)
    features = noise(key_list[0], (NODES, F), 1.0, 6.0, ((0, 256),))
    w_self = noise(key_list[1], (F, F), F ** -0.5, 0.375)
    w_neigh = noise(key_list[2], (F, F), F ** -0.5, 0.375)
    bias = noise(key_list[3], (F,), 0.5, 3.0, (), jnp.float32)
    cotangent = noise(key_list[4], (NODES, F), 1.0, 6.0, ((0, 256),))
    tile_values = draw_tile_values(jax.random.fold_in(key_list[9], 71), 0)
    tile_rows = draw_tile_rows(jax.random.fold_in(key_list[9], 71), 0)
    tile_cols = draw_tile_cols(jax.random.fold_in(key_list[9], 71), 0)
    tile_counts = draw_tile_counts(jax.random.fold_in(key_list[9], 71), 0)
    return {"features": features, "w_self": w_self, "w_neigh": w_neigh, "bias": bias, "cotangent": cotangent, "tile_values": tile_values, "tile_rows": tile_rows, "tile_cols": tile_cols, "tile_counts": tile_counts}


def reference(features, w_self, w_neigh, bias, cotangent, tile_values, tile_rows, tile_cols, tile_counts):
    blocks = features.reshape(N_BLK, N_REP, ROWT, TILE, F)
    column_ids = jnp.arange(N_BLK, dtype=jnp.int32)[:, None]
    slot_ids = jnp.arange(SLOTS, dtype=jnp.int32)[None, :]

    def partial_of(bidx, ridx):
        alive = slot_ids < tile_counts[bidx, ridx][:, None]
        gathered = blocks[column_ids, ridx, tile_cols[bidx, ridx]]
        prod = jnp.einsum('csij,csjf->csif', tile_values[bidx, ridx].astype(jnp.float32), gathered.astype(jnp.float32))
        prod = jnp.where(alive[:, :, None, None], prod, 0.0)
        total = jnp.zeros((N_REP * ROWT, TILE, F), jnp.float32)
        return total.at[tile_rows[bidx, ridx].reshape(-1)].add(prod.reshape(N_BLK * SLOTS, TILE, F))

    def agg_block(bidx):
        def per_slice(total, ridx):
            part = lax.optimization_barrier(partial_of(bidx, ridx).astype(jnp.bfloat16))
            return total + part.astype(jnp.float32), None
        total, unused = lax.scan(per_slice, jnp.zeros((N_REP * ROWT, TILE, F), jnp.float32), jnp.arange(N_REP, dtype=jnp.int32))
        return total

    agg = lax.map(agg_block, jnp.arange(N_BLK, dtype=jnp.int32)).reshape(NODES, F).astype(jnp.bfloat16)
    zvals = jnp.dot(features, w_self, preferred_element_type=jnp.float32) + jnp.dot(agg, w_neigh, preferred_element_type=jnp.float32) + bias
    sig = jax.nn.sigmoid(zvals)
    output = (zvals * sig).astype(jnp.bfloat16)
    dz = (cotangent.astype(jnp.float32) * sig * (1.0 + zvals * (1.0 - sig))).astype(jnp.bfloat16)
    grad_self = jnp.dot(features.T, dz, preferred_element_type=jnp.float32)
    grad_neigh = jnp.dot(agg.T, dz, preferred_element_type=jnp.float32)
    grad_bias = jnp.sum(dz.astype(jnp.float32), axis=0)
    dagg = jnp.dot(dz, w_neigh.T, preferred_element_type=jnp.float32).astype(jnp.bfloat16)
    dagg_blocks = dagg.reshape(N_BLK, N_REP * ROWT, TILE, F)

    def back_step(total, index):
        bidx = index // N_REP
        ridx = index % N_REP
        alive = slot_ids < tile_counts[bidx, ridx][:, None]
        picked = dagg_blocks[bidx][tile_rows[bidx, ridx]]
        term = jnp.einsum('csji,csjf->csif', tile_values[bidx, ridx].astype(jnp.float32), picked.astype(jnp.float32))
        term = jnp.where(alive[:, :, None, None], term, 0.0)
        placed = jnp.zeros((N_BLK, ROWT, TILE, F), jnp.float32).at[column_ids, tile_cols[bidx, ridx]].add(term)
        placed = lax.optimization_barrier(placed.astype(jnp.bfloat16)).astype(jnp.float32)
        return total.at[:, ridx].add(placed), None

    spread, unused = lax.scan(back_step, jnp.zeros((N_BLK, N_REP, ROWT, TILE, F), jnp.float32), jnp.arange(N_BLK * N_REP, dtype=jnp.int32))
    own = jnp.dot(dz, w_self.T, preferred_element_type=jnp.float32)
    grad_features = (own + spread.reshape(NODES, F)).astype(jnp.bfloat16)
    return output, grad_features, grad_self, grad_neigh, grad_bias
```

```python
import jax
import jax.numpy as jnp
from jax import lax
from jax.experimental import pallas as pl
from jax.experimental.pallas import tpu as pltpu
from jax.sharding import PartitionSpec as P

F32 = jnp.float32
BF16 = jnp.bfloat16
NZ, NYL, NYH, NX, NC = 8, 2, 2, 4, 2
TILE = 128
GROUP = 4
SMEM = pl.BlockSpec(memory_space=pltpu.SMEM)
VMEM = pl.BlockSpec(memory_space=pltpu.VMEM)
MB = 1024 * 1024


def permute(value, dz=0, dyl=0, dyh=0, dx=0, dc=0):
    pairs = []
    for z in range(NZ):
        for yl in range(NYL):
            for yh in range(NYH):
                for x in range(NX):
                    for c in range(NC):
                        src = (((z * NYL + yl) * NYH + yh) * NX + x) * NC + c
                        dst = (
                            (((z + dz) % NZ * NYL + (yl + dyl) % NYL) * NYH + (yh + dyh) % NYH) * NX
                            + (x + dx) % NX
                        ) * NC + (c + dc) % NC
                        pairs.append((src, dst))
    return lax.ppermute(value, ("blk", "rep"), pairs)


def params(mib):
    return pltpu.CompilerParams(vmem_limit_bytes=mib * MB)


def placed_group(a_ref, cols_ref, c, g):
    parts = []
    for k in range(GROUP):
        s = g * GROUP + k
        t = a_ref[c, s]
        col = cols_ref[c, s]
        zero = jnp.zeros_like(t)
        parts.append(
            jnp.concatenate([jnp.where(col == 0, t, zero), jnp.where(col == 1, t, zero)], axis=1)
        )
    return jnp.concatenate(parts, axis=0)


def forward_body(n, first, last, cidx_ref, rows_ref, cols_ref, cnt_ref, a_ref, *refs):
    x_refs = refs[:n]
    if first:
        acc_ref = refs[n]
        acc_ref[...] = jnp.zeros_like(acc_ref)
    else:
        acc_in, out_ref, acc_ref = refs[n : n + 3]
        acc_ref[...] = acc_in[...]
    slots = rows_ref.shape[1]
    for i in range(n):
        c = cidx_ref[i]
        for g in range(slots // GROUP):

            @pl.when(cnt_ref[c] > g * GROUP)
            def _():
                lhs = placed_group(a_ref, cols_ref, c, g)
                prod = jnp.dot(lhs, x_refs[i][...], preferred_element_type=F32)
                for k in range(GROUP):
                    acc_ref[rows_ref[c, g * GROUP + k]] += prod[k * TILE : (k + 1) * TILE]

    if last:
        for q in range(out_ref.shape[0]):
            out_ref[q] = acc_ref[q].astype(BF16)


def forward_kernel(cidx, rows, cols, cnt, values, blocks, acc=None):
    n = len(blocks)
    width = blocks[0].shape[1]
    tiles = NYH * NX * NC * 2
    shape = (tiles, TILE, width)
    first = acc is None
    ins = [cidx, rows, cols, cnt, values, *blocks]
    if not first:
        ins.append(acc)

    def body(*refs):
        forward_body(n, first, not first, *refs)

    return pl.pallas_call(
        body,
        out_shape=jax.ShapeDtypeStruct(shape, F32 if first else BF16),
        in_specs=[SMEM] * 4 + [VMEM] * (len(ins) - 4),
        out_specs=VMEM,
        scratch_shapes=[] if first else [pltpu.VMEM(shape, F32)],
        compiler_params=params(24),
        cost_estimate=pl.CostEstimate(
            flops=2 * n * 12 * TILE * 256 * width, bytes_accessed=n * 12 * TILE * TILE * 2, transcendentals=0
        ),
    )(*ins)


def backward_body(n, cidx_ref, rows_ref, cols_ref, cnt_ref, a_ref, g_ref, *refs):
    outs = refs[:n]
    acc_ref = refs[n]
    slots = rows_ref.shape[1]
    for i in range(n):
        c = cidx_ref[i]
        acc_ref[...] = jnp.zeros_like(acc_ref)
        for g in range(slots // GROUP):

            @pl.when(cnt_ref[c] > g * GROUP)
            def _():
                rhs = placed_group(a_ref, cols_ref, c, g)
                lhs = jnp.concatenate(
                    [g_ref[rows_ref[c, g * GROUP + k]] for k in range(GROUP)], axis=1
                )
                acc_ref[...] += jnp.dot(lhs, rhs, preferred_element_type=F32)

        outs[i][...] = acc_ref[...].astype(BF16)


def backward_kernel(cidx, rows, cols, cnt, values, grad_tiles, n):
    width = grad_tiles.shape[1]

    def body(*refs):
        backward_body(n, *refs)

    return pl.pallas_call(
        body,
        out_shape=[jax.ShapeDtypeStruct((width, 2 * TILE), BF16)] * n,
        in_specs=[SMEM] * 4 + [VMEM] * 2,
        out_specs=[VMEM] * n,
        scratch_shapes=[pltpu.VMEM((width, 2 * TILE), F32)],
        compiler_params=params(24),
        cost_estimate=pl.CostEstimate(
            flops=2 * n * 12 * TILE * 256 * width, bytes_accessed=n * 12 * TILE * TILE * 2, transcendentals=0
        ),
    )(cidx, rows, cols, cnt, values, grad_tiles)


NT = (((1,), (1,)), ((), ()))
TN = (((0,), (0,)), ((), ()))


def dense_body(x_ref, a0_ref, a1_ref, cot_ref, ws_ref, wn_ref, bias_ref, out_ref, dz_ref, agg_ref, dagg_ref):
    agg = (a0_ref[...].astype(F32) + a1_ref[...].astype(F32)).astype(BF16)
    agg_ref[...] = agg
    z = (
        jnp.dot(x_ref[...], ws_ref[...], preferred_element_type=F32)
        + jnp.dot(agg, wn_ref[...], preferred_element_type=F32)
        + bias_ref[...]
    )
    sig = jax.nn.sigmoid(z)
    out_ref[...] = (z * sig).astype(BF16)
    dz = (cot_ref[...].astype(F32) * sig * (1.0 + z * (1.0 - sig))).astype(BF16)
    dz_ref[...] = dz
    dagg = lax.dot_general(wn_ref[...], dz, NT, preferred_element_type=F32).astype(BF16)
    for t in range(2):
        dagg_ref[t] = dagg[:, t * TILE : (t + 1) * TILE]


def dense_kernel(x, a0, a1, cot, w_self, w_neigh, bias):
    n, f = x.shape
    return pl.pallas_call(
        dense_body,
        out_shape=[jax.ShapeDtypeStruct((n, f), BF16)] * 3 + [jax.ShapeDtypeStruct((2, f, TILE), BF16)],
        in_specs=[VMEM] * 7,
        out_specs=[VMEM] * 4,
        compiler_params=params(16),
    )(x, a0, a1, cot, w_self, w_neigh, bias)


def weight_body(place_ref, x_ref, agg_ref, dz_ref, ws_ref, parts_ref, own_ref):
    dz = dz_ref[...]
    gs = lax.dot_general(x_ref[...], dz, TN, preferred_element_type=F32)
    gn = lax.dot_general(agg_ref[...], dz, TN, preferred_element_type=F32)
    gb = jnp.sum(dz.astype(F32), axis=0, keepdims=True)
    for p in range(16):
        src = gs if p < 8 else gn
        o = (p % 8) * 32
        at = place_ref[p]
        parts_ref[at, 0:32, :] = src[o : o + 32].astype(BF16)
        parts_ref[at, 32:48, :] = jnp.broadcast_to(gb, (16, gb.shape[1])).astype(BF16)
    own_ref[...] = lax.dot_general(dz, ws_ref[...], NT, preferred_element_type=F32)


def weight_kernel(place, x, agg, dz, w_self):
    n, f = x.shape
    return pl.pallas_call(
        weight_body,
        out_shape=[jax.ShapeDtypeStruct((16, 48, f), BF16), jax.ShapeDtypeStruct((n, f), F32)],
        in_specs=[SMEM] + [VMEM] * 4,
        out_specs=[VMEM] * 2,
        compiler_params=params(16),
    )(place, x, agg, dz, w_self)


def final_body(place_ref, own_ref, t_ref, r0_ref, r1_ref, y_ref, parts_ref, gf_ref, gs_ref, gn_ref, gb_ref):
    spread = (
        t_ref[...].astype(F32) + r0_ref[...].astype(F32) + r1_ref[...].astype(F32) + y_ref[...].astype(F32)
    )
    gf_ref[...] = (own_ref[...] + spread.T).astype(BF16)
    for p in range(16):
        dst = gs_ref if p < 8 else gn_ref
        o = (p % 8) * 32
        dst[o : o + 32, :] = parts_ref[place_ref[p], 0:32, :].astype(F32)
    gb_ref[...] = parts_ref[place_ref[0], 32:48, :].astype(F32)


def final_kernel(place, own, t, r0, r1, y, parts):
    n, f = own.shape
    sq = jax.ShapeDtypeStruct((f, f), F32)
    return pl.pallas_call(
        final_body,
        out_shape=[jax.ShapeDtypeStruct((n, f), BF16), sq, sq, jax.ShapeDtypeStruct((16, f), F32)],
        in_specs=[SMEM] + [VMEM] * 6,
        out_specs=[VMEM] * 4,
        compiler_params=params(16),
    )(place, own, t, r0, r1, y, parts)


def add(*terms):
    total = terms[0].astype(F32)
    for t in terms[1:]:
        total = total + t.astype(F32)
    return total


def local(features, w_self, w_neigh, bias, cotangent, tile_values, tile_rows, tile_cols, tile_counts):
    values = tile_values[0, 0]
    counts = tile_counts[0, 0]
    slots = values.shape[1]
    bi = lax.axis_index("blk")
    ri = lax.axis_index("rep")
    z, yl = bi // 2, bi % 2
    yh, x, core = ri // 8, (ri // 2) % 4, ri % 2

    def place_of(q):
        return (((q % 2 + core) % 2) * 4 + (q // 2 + 4 - x) % 4) * 2 + (q // 8 + yh) % 2

    rows = place_of(tile_rows[0, 0] // 2) * 2 + tile_rows[0, 0] % 2
    live = lax.broadcasted_iota(jnp.int32, (16, slots), 1) < counts[:, None]
    cols = jnp.where(live, tile_cols[0, 0], 2)
    place = place_of(jnp.arange(16, dtype=jnp.int32))

    def blocks_at(offsets):
        return jnp.stack([(z + dz + NZ) % NZ * 2 + (yl + dy) % 2 for dz, dy in offsets]).astype(jnp.int32)

    got = {(0, 0): features}
    got[0, 1] = permute(features, dyl=1)
    for k in (1, 2, 3):
        for dy in (0, 1):
            got[-k, dy] = permute(got[1 - k, dy], dz=1)
            got[k, dy] = permute(got[k - 1, dy], dz=-1)
    got[4, 0] = permute(got[-3, 0], dz=1)
    got[4, 1] = permute(got[3, 1], dz=-1)
    near = [(k, dy) for k in (0, 1, -1, 2, -2) for dy in (0, 1)]
    far = [(k, dy) for k in (3, -3, 4) for dy in (0, 1)]
    meta = (rows, cols, counts, values)
    acc = forward_kernel(blocks_at(near), *meta, [got[o] for o in near])
    partial = forward_kernel(blocks_at(far), *meta, [got[o] for o in far], acc)

    width = features.shape[1]
    partial = partial.reshape(2, 16 * TILE, width)
    half = add(partial[0], permute(partial[1], dc=1)).astype(BF16).reshape(4, 4 * TILE, width)
    quarter = add(
        half[0], permute(half[1], dx=1), permute(half[3], dx=-1), permute(half[2], dx=2)
    ).astype(BF16).reshape(2, 2 * TILE, width)
    other = permute(quarter[1], dyh=1)

    output, dz, agg, dagg = dense_kernel(
        features, quarter[0], other, cotangent, w_self, w_neigh, bias.reshape(1, width)
    )

    pair = jnp.concatenate([dagg, permute(dagg, dyh=1)], axis=0)
    from_left = permute(pair, dx=1)
    from_right = permute(pair, dx=-1)
    from_across = permute(pair, dx=2)
    mine = jnp.concatenate([pair, from_right, from_across, from_left], axis=0)
    grad_tiles = jnp.concatenate([mine, permute(mine, dc=1)], axis=0)

    parts, own = weight_kernel(place, features, agg, dz, w_self)

    parts = parts.reshape(2, 8, 48, width)
    w = add(parts[0], permute(parts[1], dc=1)).astype(BF16).reshape(4, 2, 48, width)
    w = add(w[0], permute(w[1], dx=1), permute(w[3], dx=-1), permute(w[2], dx=2)).astype(BF16)
    w = add(w[0], permute(w[1], dyh=1))
    w = w + permute(w, dyl=1)
    for bit in (1, 2, 4):
        w = w + exchange_z(w, bit)
    w = w.astype(BF16)[None]
    w = jnp.concatenate([w, permute(w, dyh=1)], axis=0)
    w = jnp.concatenate([w, permute(w, dx=-1), permute(w, dx=2), permute(w, dx=1)], axis=0)
    w = jnp.concatenate([w, permute(w, dc=1)], axis=0)

    order = [(4, 0), (4, 1), (3, 0), (-3, 0), (3, 1), (-3, 1)]
    rest = [(k, dy) for k in (2, -2, 1, -1, 0) for dy in (1, 0)]
    terms = dict(zip(order, backward_kernel(blocks_at(order), *meta, grad_tiles, len(order))))
    terms.update(zip(rest, backward_kernel(blocks_at(rest), *meta, grad_tiles, len(rest))))

    def ring(dy, sign, start):
        moving = permute(terms[4 if start == 4 else sign * start, dy], dz=sign)
        for k in range(start - 1, 0, -1):
            moving = permute(add(terms[sign * k, dy], moving).astype(BF16), dz=sign)
        return moving

    q_up, q_down = ring(1, 1, 3), ring(1, -1, 4)
    o_up, o_down = ring(0, 1, 4), ring(0, -1, 3)
    theirs = add(terms[0, 1], q_up, q_down).astype(BF16)
    grad_features, grad_self, grad_neigh, grad_bias = final_kernel(
        place, own, terms[0, 0], o_up, o_down, permute(theirs, dyl=1), w
    )
    return (output, grad_features, grad_self, grad_neigh, grad_bias[0])


def exchange_z(value, bit):
    pairs = []
    for z in range(NZ):
        for rest in range(NYL * NYH * NX * NC):
            pairs.append((z * 32 + rest, (z ^ bit) * 32 + rest))
    return lax.ppermute(value, ("blk", "rep"), pairs)


def solution(mesh):
    in_specs = (
        P(("blk", "rep"), None),
        P(),
        P(),
        P(),
        P(("blk", "rep"), None),
        P("blk", "rep", None, None, None, None),
        P("blk", "rep", None, None),
        P("blk", "rep", None, None),
        P("blk", "rep", None),
    )
    out_specs = (P(("blk", "rep"), None), P(("blk", "rep"), None), P(), P(), P())
    return jax.shard_map(local, mesh=mesh, in_specs=in_specs, out_specs=out_specs, check_vma=False)
```

```python
import jax
import jax.numpy as jnp
from jax import lax
from jax.experimental import pallas as pl
from jax.experimental.pallas import tpu as pltpu
from jax.sharding import PartitionSpec as P

F32 = jnp.float32
BF16 = jnp.bfloat16
NZ, NYL, NYH, NX, NC = 8, 2, 2, 4, 2
TILE = 128
SMEM = pl.BlockSpec(memory_space=pltpu.SMEM)
VMEM = pl.BlockSpec(memory_space=pltpu.VMEM)
MB = 1024 * 1024


def permute(value, dz=0, dyl=0, dyh=0, dx=0, dc=0):
    pairs = []
    for z in range(NZ):
        to_z = (z + (dz(z) if callable(dz) else dz)) % NZ
        for yl in range(NYL):
            for yh in range(NYH):
                for x in range(NX):
                    to_x = (x + (dx(x) if callable(dx) else dx)) % NX
                    for c in range(NC):
                        src = (((z * NYL + yl) * NYH + yh) * NX + x) * NC + c
                        dst = (((to_z * NYL + (yl + dyl) % NYL) * NYH + (yh + dyh) % NYH) * NX + to_x) * NC
                        pairs.append((src, dst + (c + dc) % NC))
    return lax.ppermute(value, ("blk", "rep"), pairs)


def params(mib):
    return pltpu.CompilerParams(vmem_limit_bytes=mib * MB)


def axes():
    b, r = lax.axis_index("blk"), lax.axis_index("rep")
    return b >> 1, b & 1, r >> 3, (r >> 1) & 3, r & 1


SETS = (
    ((0, 0), (0, 1), (1, 0), (1, 1), (-1, 0), (-1, 1)),
    ((2, 0), (2, 1), (-2, 0), (-2, 1)),
    ((3, 0), (3, 1), (-3, 0), (-3, 1)),
    ((4, 0), (4, 1)),
)
UNROLL = 16
LIST = 6 * 12 + UNROLL
ROW_TILES = 32


def list_body(rows_ref, cols_ref, cnt_ref, list_ref, len_ref):
    z, yl, yh, x, core = axes()
    slots = rows_ref.shape[1]
    for k, offsets in enumerate(SETS):
        n = jnp.int32(0)
        for i, (dz, dy) in enumerate(offsets):
            c = ((z + dz + NZ) & (NZ - 1)) * 2 + (yl ^ dy)

            def put(s, _, c=c, i=i, k=k, n=n):
                row = rows_ref[c, s]
                q = row >> 1
                place = (((q & 1) ^ core) * 4 + (((q >> 1) - x) & 3)) * 2 + ((q >> 3) ^ yh)
                place = place * 2 + (row & 1)
                near = i * 2 + cols_ref[c, s]
                list_ref[k, n + s] = (c * slots + s) | (near << 8) | (place << 16)
                return 0

            lax.fori_loop(0, cnt_ref[c], put, 0)
            n = n + cnt_ref[c]
        len_ref[k] = (n + UNROLL - 1) // UNROLL
        for s in range(UNROLL):
            list_ref[k, n + s] = ((2 * len(offsets)) << 8) | (ROW_TILES << 16)


def list_kernel(rows, cols, counts):
    return pl.pallas_call(
        list_body,
        out_shape=[
            jax.ShapeDtypeStruct((len(SETS), LIST), jnp.int32),
            jax.ShapeDtypeStruct((len(SETS),), jnp.int32),
        ],
        in_specs=[SMEM] * 3,
        out_specs=[SMEM] * 2,
        compiler_params=params(16),
    )(rows, cols, counts)


def load_kernel(values):
    def body(hbm, out, sem):
        copy = pltpu.make_async_copy(hbm, out, sem)
        copy.start()
        copy.wait()

    return pl.pallas_call(
        body,
        out_shape=jax.ShapeDtypeStruct(values.shape, values.dtype),
        in_specs=[pl.BlockSpec(memory_space=pltpu.HBM)],
        out_specs=VMEM,
        scratch_shapes=[pltpu.SemaphoreType.DMA],
        compiler_params=params(16),
    )(values)


def each_tile(k, list_ref, len_ref, step):
    def some(j, _):
        for u in range(UNROLL):
            e = list_ref[k, j * UNROLL + u]
            step(e & 255, (e >> 8) & 255, e >> 16)
        return 0

    lax.fori_loop(0, len_ref[k], some, 0)


def bases(sets):
    at, out = 0, []
    for k in sets:
        out.append(at)
        at += 2 * len(SETS[k]) + 1
    return out, at


def forward_kernel(sets, lists, lens, tiles, got, acc, last):
    blocks = [got[o] for k in sets for o in SETS[k]]
    n = len(blocks)
    width = blocks[0].shape[1]
    shape = (ROW_TILES + 1, TILE, width)
    starts, total = bases(sets)

    def body(list_ref, len_ref, a_ref, *refs):
        x_refs, rest = refs[:n], refs[n:]
        x_all = rest[-1]
        acc_ref = rest[-2]
        if acc is None:
            acc_ref[...] = jnp.zeros_like(acc_ref)
        else:
            acc_ref[...] = rest[0][...]
        x_iter = iter(x_refs)
        for k, start in zip(sets, starts):
            for i in range(len(SETS[k])):
                ref = next(x_iter)
                for t in range(2):
                    x_all[start + 2 * i + t] = ref[t * TILE : (t + 1) * TILE, :]
            x_all[start + 2 * len(SETS[k])] = jnp.zeros_like(x_all[0])
        for k, start in zip(sets, starts):

            def step(tile, near, place, start=start):
                acc_ref[place] += jnp.dot(a_ref[tile], x_all[start + near], preferred_element_type=F32)

            each_tile(k, list_ref, len_ref, step)
        if last:
            out_ref = rest[-3]
            for p in range(ROW_TILES):
                out_ref[p] = acc_ref[p].astype(BF16)

    ins = [lists, lens, tiles, *blocks] + ([] if acc is None else [acc])
    scratch = [pltpu.VMEM((total, TILE, width), BF16)]
    if last:
        out_shape = jax.ShapeDtypeStruct((ROW_TILES, TILE, width), BF16)
        scratch = [pltpu.VMEM(shape, F32)] + scratch
    else:
        out_shape = jax.ShapeDtypeStruct(shape, F32)
    return pl.pallas_call(
        body,
        out_shape=out_shape,
        in_specs=[SMEM] * 2 + [VMEM] * (len(ins) - 2),
        out_specs=VMEM,
        scratch_shapes=scratch,
        compiler_params=params(16),
        cost_estimate=pl.CostEstimate(
            flops=2 * n * 12 * TILE * TILE * width, bytes_accessed=n * 5 * TILE * TILE * 2, transcendentals=0
        ),
    )(*ins)


def backward_kernel(k, lists, lens, tiles, mine, theirs):
    n = len(SETS[k]) // 2
    width = mine.shape[1]

    def body(list_ref, len_ref, a_ref, mine_ref, their_ref, *refs):
        outs, other, (g_all, acc_ref) = refs[:n], refs[n], refs[n + 1 :]
        half = ROW_TILES // 2
        g_all[0:half] = mine_ref[...]
        g_all[half : 2 * half] = their_ref[...]
        g_all[2 * half] = jnp.zeros_like(g_all[2 * half])
        acc_ref[...] = jnp.zeros_like(acc_ref)

        def step(tile, near, place):
            acc_ref[near] += jnp.dot(g_all[place], a_ref[tile], preferred_element_type=F32)

        each_tile(k, list_ref, len_ref, step)
        for i in range(n):
            for t in range(2):
                outs[i][:, t * TILE : (t + 1) * TILE] = acc_ref[4 * i + t].astype(BF16)
                other[i, :, t * TILE : (t + 1) * TILE] = acc_ref[4 * i + 2 + t].astype(BF16)

    result = pl.pallas_call(
        body,
        out_shape=[jax.ShapeDtypeStruct((width, 2 * TILE), BF16)] * n
        + [jax.ShapeDtypeStruct((n, width, 2 * TILE), BF16)],
        in_specs=[SMEM] * 2 + [VMEM] * 3,
        out_specs=[VMEM] * (n + 1),
        scratch_shapes=[
            pltpu.VMEM((ROW_TILES + 1, width, TILE), BF16),
            pltpu.VMEM((4 * n + 1, width, TILE), F32),
        ],
        compiler_params=params(16),
        cost_estimate=pl.CostEstimate(
            flops=4 * n * 12 * TILE * TILE * width, bytes_accessed=n * 10 * TILE * TILE * 2, transcendentals=0
        ),
    )(lists, lens, tiles, mine, theirs)
    return result[:n], result[n]


def join_kernel(pieces):
    sizes = [p.shape[0] for p in pieces]

    def body(*refs):
        at = 0
        for ref, size in zip(refs, sizes):
            refs[-1][at : at + size] = ref[...]
            at += size

    return pl.pallas_call(
        body,
        out_shape=jax.ShapeDtypeStruct((sum(sizes),) + pieces[0].shape[1:], pieces[0].dtype),
        in_specs=[VMEM] * len(pieces),
        out_specs=VMEM,
        compiler_params=params(16),
    )(*pieces)


NT = (((1,), (1,)), ((), ()))
TN = (((0,), (0,)), ((), ()))


def dense_body(x_ref, a0_ref, a1_ref, cot_ref, ws_ref, wn_ref, bias_ref, out_ref, dz_ref, agg_ref, dagg_ref):
    agg = (a0_ref[...].astype(F32) + a1_ref[...].astype(F32)).astype(BF16)
    agg_ref[...] = agg
    z = (
        jnp.dot(x_ref[...], ws_ref[...], preferred_element_type=F32)
        + jnp.dot(agg, wn_ref[...], preferred_element_type=F32)
        + bias_ref[...]
    )
    sig = jax.nn.sigmoid(z)
    out_ref[...] = (z * sig).astype(BF16)
    dz = (cot_ref[...].astype(F32) * sig * (1.0 + z * (1.0 - sig))).astype(BF16)
    dz_ref[...] = dz
    dagg = lax.dot_general(wn_ref[...], dz, NT, preferred_element_type=F32).astype(BF16)
    for t in range(2):
        dagg_ref[t] = dagg[:, t * TILE : (t + 1) * TILE]


def dense_kernel(x, a0, a1, cot, w_self, w_neigh, bias):
    n, f = x.shape
    return pl.pallas_call(
        dense_body,
        out_shape=[jax.ShapeDtypeStruct((n, f), BF16)] * 3 + [jax.ShapeDtypeStruct((2, f, TILE), BF16)],
        in_specs=[VMEM] * 7,
        out_specs=[VMEM] * 4,
        compiler_params=params(16),
    )(x, a0, a1, cot, w_self, w_neigh, bias)


PART = 256 + 16


def weight_body(x_ref, agg_ref, dz_ref, ws_ref, parts_ref, own_ref):
    z, yl, yh, x, core = axes()
    dz = dz_ref[...]
    gb = jnp.sum(dz.astype(F32), axis=0, keepdims=True)
    bias = jnp.broadcast_to(gb, (16, gb.shape[1])).astype(BF16)
    for h, ref in enumerate((x_ref, agg_ref)):
        grad = lax.dot_general(ref[...], dz, TN, preferred_element_type=F32).astype(BF16)
        parts_ref[core ^ h, 0:256, :] = grad
        parts_ref[core ^ h, 256:PART, :] = bias
    own_ref[...] = lax.dot_general(dz, ws_ref[...], NT, preferred_element_type=F32)


def weight_kernel(x, agg, dz, w_self):
    n, f = x.shape
    return pl.pallas_call(
        weight_body,
        out_shape=[jax.ShapeDtypeStruct((2, PART, f), BF16), jax.ShapeDtypeStruct((n, f), F32)],
        in_specs=[VMEM] * 4,
        out_specs=[VMEM] * 2,
        compiler_params=params(16),
    )(x, agg, dz, w_self)


def hop_kernel(terms, moving, w):
    refs = [t[0] if isinstance(t, tuple) else t for t in terms]
    at = [t[1] if isinstance(t, tuple) else None for t in terms]
    rows, width = refs[0].shape[-2:]

    def body(*refs):
        out, rider = refs[-1], refs[-2]
        total = None
        for ref, i in zip(refs, at):
            term = (ref[...] if i is None else ref[i]).astype(F32)
            total = term if total is None else total + term
        if moving is None:
            out[rows:, :] = rider[...]
        else:
            total = total + rider[0:rows, :].astype(F32)
            out[rows:, :] = rider[rows:, :]
        out[0:rows, :] = total.astype(BF16)

    ins = refs + [w if moving is None else moving]
    return pl.pallas_call(
        body,
        out_shape=jax.ShapeDtypeStruct((rows + PART, width), BF16),
        in_specs=[VMEM] * len(ins),
        out_specs=VMEM,
        compiler_params=params(16),
    )(*ins)


def total_kernel(w, ups, downs):
    n = len(ups) + len(downs) + 1
    rows = ups[0].shape[0] - PART

    def body(*refs):
        out, all_ref = refs[-2:]
        z = axes()[0]
        all_ref[z] = refs[0][...]
        for j in range(len(ups)):
            all_ref[(z - 1 - j) & (NZ - 1)] = refs[1 + j][rows:, :]
        for j in range(len(downs)):
            all_ref[(z + 1 + j) & (NZ - 1)] = refs[1 + len(ups) + j][rows:, :]
        total = all_ref[0].astype(F32)
        for i in range(1, NZ):
            total = total + all_ref[i].astype(F32)
        out[...] = total.astype(BF16)

    return pl.pallas_call(
        body,
        out_shape=jax.ShapeDtypeStruct(w.shape, BF16),
        in_specs=[VMEM] * n,
        out_specs=VMEM,
        scratch_shapes=[pltpu.VMEM((NZ,) + w.shape, BF16)],
        compiler_params=params(16),
    )(w, *ups, *downs)


def final_body(own_ref, t_ref, up_ref, down_ref, y_ref, w0_ref, w1_ref, gf_ref, gs_ref, gn_ref, gb_ref):
    core = axes()[4]
    f = t_ref.shape[0]
    spread = (
        t_ref[...].astype(F32) + up_ref[0:f, :].astype(F32) + down_ref[0:f, :].astype(F32) + y_ref[...].astype(F32)
    )
    gf_ref[...] = (own_ref[...] + spread.T).astype(BF16)

    def write(first, second):
        gs_ref[...] = first[0:f, :].astype(F32)
        gn_ref[...] = second[0:f, :].astype(F32)
        gb_ref[...] = first[f:PART, :].astype(F32)[0:1]

    pl.when(core == 0)(lambda: write(w0_ref, w1_ref))
    pl.when(core == 1)(lambda: write(w1_ref, w0_ref))


def final_kernel(own, t, up, down, y, w0, w1):
    n, f = own.shape
    sq = jax.ShapeDtypeStruct((f, f), F32)
    return pl.pallas_call(
        final_body,
        out_shape=[jax.ShapeDtypeStruct((n, f), BF16), sq, sq, jax.ShapeDtypeStruct((1, f), F32)],
        in_specs=[VMEM] * 7,
        out_specs=[VMEM] * 4,
        compiler_params=params(16),
    )(own, t, up, down, y, w0, w1)


def add(*terms):
    total = terms[0].astype(F32)
    for t in terms[1:]:
        total = total + t.astype(F32)
    return total.astype(BF16)


def flip_z(value, bit):
    return permute(value, dz=lambda z: (z ^ bit) - z)


def after(value, *done):
    return lax.optimization_barrier((value, *done))[0]


def local(features, w_self, w_neigh, bias, cotangent, tile_values, tile_rows, tile_cols, tile_counts):
    width = features.shape[1]
    lists, lens = list_kernel(tile_rows[0, 0], tile_cols[0, 0], tile_counts[0, 0])
    tiles = load_kernel(tile_values.reshape((-1,) + tile_values.shape[4:]))

    together = lax.optimization_barrier
    up, down = permute(features, dz=1), permute(features, dz=-1)
    got = {(0, 0): features}
    up, down, got[0, 1], lists = together((up, down, permute(features, dyl=1), lists))
    acc = None
    for k in (1, 2, 3, 4):
        got[-k, 0], got[k, 0] = up, down
        here = (up, down)
        if k < 3:
            up, down = permute(up, dz=1), permute(down, dz=-1)
        elif k == 3:
            up = down = permute(up, dz=1)
        there = permute(join_kernel(here) if k < 4 else up, dyl=1)
        if k == 1:
            up, down, there, tiles = together((up, down, there, tiles))
        else:
            acc = forward_kernel((k - 2,), lists, lens, tiles, got, acc, False)
            up, down, there, acc = together((up, down, there, acc))
        rows = features.shape[0]
        got[-k, 1], got[k, 1] = (there[:rows], there[rows:]) if k < 4 else (there, there)
    partial = forward_kernel((3,), lists, lens, tiles, got, acc, True)

    partial = partial.reshape(2, 16 * TILE, width)
    half = add(partial[0], permute(partial[1], dc=1)).reshape(4, 4 * TILE, width)
    quarter = add(
        half[0], permute(half[1], dx=1), permute(half[3], dx=-1), permute(half[2], dx=2)
    ).reshape(2, 2 * TILE, width)
    other = permute(quarter[1], dyh=1)

    output, dz, agg, dagg = dense_kernel(
        features, quarter[0], other, cotangent, w_self, w_neigh, bias.reshape(1, width)
    )

    parts, own = weight_kernel(features, agg, dz, w_self)
    w = add(parts[0], permute(parts[1], dc=1))
    dagg_y, w = together((permute(dagg, dyh=1), w))
    pair = join_kernel([dagg, dagg_y])
    w = add(w, permute(w, dyl=1))
    from_left, from_right, w = together((permute(pair, dx=1), permute(pair, dx=-1), w))
    w = add(w, permute(w, dyh=1))
    left, right, w = together((permute(from_left[0:2], dx=1), permute(from_right[2:4], dx=-1), w))
    mine = join_kernel([pair, from_right, left, right, from_left])
    w = add(w, permute(w, dx=lambda x: (x ^ 1) - x))
    theirs, w = together((permute(mine, dc=1), w))

    def products(k):
        return backward_kernel(k, lists, lens, tiles, mine, theirs)

    (t4,), u4 = products(3)
    w, theirs, u4 = together((w, theirs, u4))
    (t3, t3d), u3 = products(2)
    y4, w, theirs, u3 = together(
        (permute(u4, dyl=1), add(w, permute(w, dx=lambda x: 3 - 2 * x)), theirs, u3)
    )
    (t2, t2d), u2 = products(1)
    up1, y3, theirs, u2 = together(
        (permute(hop_kernel([t4, (y4, 0)], None, w), dz=1), permute(u3, dyl=1), theirs, u2)
    )
    (t0, t1, t1d), u1 = products(0)
    up2, down1, y2, u1 = together(
        (
            permute(hop_kernel([t3, (y3, 0)], up1, w), dz=1),
            permute(hop_kernel([t3d, (y3, 1)], None, w), dz=-1),
            permute(u2, dyl=1),
            u1,
        )
    )
    up3, down2, y1 = together(
        (
            permute(hop_kernel([t2, (y2, 0)], up2, w), dz=1),
            permute(hop_kernel([t2d, (y2, 1)], down1, w), dz=-1),
            permute(u1[1:], dyl=1),
        )
    )
    up4, down3, y0 = together(
        (
            permute(hop_kernel([t1, (y1, 0)], up3, w), dz=1),
            permute(hop_kernel([t1d, (y1, 1)], down2, w), dz=-1),
            permute(u1[0], dyl=1),
        )
    )
    w = total_kernel(w, [up1, up2, up3, up4], [down1, down2, down3])
    grad_features, grad_self, grad_neigh, grad_bias = final_kernel(
        own, t0, up4, down3, y0, w, permute(w, dc=1)
    )
    return (output, grad_features, grad_self, grad_neigh, grad_bias.reshape(width))


def solution(mesh):
    in_specs = (
        P(("blk", "rep"), None),
        P(),
        P(),
        P(),
        P(("blk", "rep"), None),
        P("blk", "rep", None, None, None, None),
        P("blk", "rep", None, None),
        P("blk", "rep", None, None),
        P("blk", "rep", None),
    )
    out_specs = (P(("blk", "rep"), None), P(("blk", "rep"), None), P(), P(), P())
    return jax.shard_map(local, mesh=mesh, in_specs=in_specs, out_specs=out_specs, check_vma=False)
```

```python
import jax
import jax.numpy as jnp
from jax import lax
from jax.experimental import pallas as pl
from jax.experimental.pallas import tpu as pltpu
from jax.sharding import PartitionSpec as P

F32 = jnp.float32
BF16 = jnp.bfloat16
NZ, NYL, NYH, NX, NC = 8, 2, 2, 4, 2
TILE = 128
SMEM = pl.BlockSpec(memory_space=pltpu.SMEM)
VMEM = pl.BlockSpec(memory_space=pltpu.VMEM)
MB = 1024 * 1024


def permute(value, dz=0, dyl=0, dyh=0, dx=0, dc=0):
    pairs = []
    for z in range(NZ):
        to_z = (z + (dz(z) if callable(dz) else dz)) % NZ
        for yl in range(NYL):
            for yh in range(NYH):
                for x in range(NX):
                    to_x = (x + (dx(x) if callable(dx) else dx)) % NX
                    for c in range(NC):
                        src = (((z * NYL + yl) * NYH + yh) * NX + x) * NC + c
                        dst = (((to_z * NYL + (yl + dyl) % NYL) * NYH + (yh + dyh) % NYH) * NX + to_x) * NC
                        pairs.append((src, dst + (c + dc) % NC))
    return lax.ppermute(value, ("blk", "rep"), pairs)


def params(mib):
    return pltpu.CompilerParams(vmem_limit_bytes=mib * MB)


def axes():
    b, r = lax.axis_index("blk"), lax.axis_index("rep")
    return b >> 1, b & 1, r >> 3, (r >> 1) & 3, r & 1


SETS = (
    ((0, 0), (0, 1), (1, 0), (1, 1), (-1, 0), (-1, 1)),
    ((2, 0), (2, 1), (-2, 0), (-2, 1)),
    ((3, 0), (3, 1), (-3, 0), (-3, 1)),
    ((4, 0), (4, 1)),
)
UNROLL = 16
LIST = 6 * 12 + UNROLL
ROW_TILES = 32


def list_body(rows_ref, cols_ref, cnt_ref, list_ref, len_ref):
    z, yl, yh, x, core = axes()
    slots = rows_ref.shape[0]
    for k, offsets in enumerate(SETS):
        n = jnp.int32(0)
        for i, (dz, dy) in enumerate(offsets):
            c = ((z + dz + NZ) & (NZ - 1)) * 2 + (yl ^ dy)

            def put(s, _, c=c, i=i, k=k, n=n):
                row = rows_ref[s, c]
                q = row >> 1
                place = ((q & 1) ^ core) * 16 + (q >> 1) * 2 + (row & 1)
                near = i * 2 + cols_ref[s, c]
                list_ref[k, n + s] = (c * slots + s) | (near << 8) | (place << 16)
                return 0

            lax.fori_loop(0, cnt_ref[c], put, 0)
            n = n + cnt_ref[c]
        len_ref[k] = (n + UNROLL - 1) // UNROLL
        for s in range(UNROLL):
            list_ref[k, n + s] = ((2 * len(offsets)) << 8) | (ROW_TILES << 16)


def list_kernel(rows, cols, counts):
    return pl.pallas_call(
        list_body,
        out_shape=[
            jax.ShapeDtypeStruct((len(SETS), LIST), jnp.int32),
            jax.ShapeDtypeStruct((len(SETS),), jnp.int32),
        ],
        in_specs=[SMEM] * 3,
        out_specs=[SMEM] * 2,
        compiler_params=params(16),
    )(rows, cols, counts)


def load_kernel(values):
    def body(hbm, out, sem):
        copy = pltpu.make_async_copy(hbm, out, sem)
        copy.start()
        copy.wait()

    return pl.pallas_call(
        body,
        out_shape=jax.ShapeDtypeStruct(values.shape, values.dtype),
        in_specs=[pl.BlockSpec(memory_space=pltpu.HBM)],
        out_specs=VMEM,
        scratch_shapes=[pltpu.SemaphoreType.DMA],
        compiler_params=params(16),
    )(values)


def each_tile(k, list_ref, len_ref, step):
    def some(j, _):
        for u in range(UNROLL):
            e = list_ref[k, j * UNROLL + u]
            step(e & 255, (e >> 8) & 255, e >> 16)
        return 0

    lax.fori_loop(0, len_ref[k], some, 0)


def bases(sets):
    at, out = 0, []
    for k in sets:
        out.append(at)
        at += 2 * len(SETS[k]) + 1
    return out, at


def forward_kernel(sets, lists, lens, tiles, got, acc, last):
    blocks = [got[o] for k in sets for o in SETS[k]]
    n = len(blocks)
    width = blocks[0].shape[1]
    shape = (ROW_TILES + 1, TILE, width)
    starts, total = bases(sets)

    def body(list_ref, len_ref, a_ref, *refs):
        x_refs, rest = refs[:n], refs[n:]
        x_all = rest[-1]
        acc_ref = rest[-2]
        if acc is None:
            acc_ref[...] = jnp.zeros_like(acc_ref)
        else:
            acc_ref[...] = rest[0][...]
        x_iter = iter(x_refs)
        for k, start in zip(sets, starts):
            for i in range(len(SETS[k])):
                ref = next(x_iter)
                for t in range(2):
                    x_all[start + 2 * i + t] = ref[t * TILE : (t + 1) * TILE, :]
            x_all[start + 2 * len(SETS[k])] = jnp.zeros_like(x_all[0])
        for k, start in zip(sets, starts):

            def step(tile, near, place, start=start):
                acc_ref[place] += jnp.dot(a_ref[tile], x_all[start + near], preferred_element_type=F32)

            each_tile(k, list_ref, len_ref, step)
        if last:
            out_ref = rest[-3]
            for p in range(ROW_TILES):
                out_ref[p] = acc_ref[p].astype(BF16)

    ins = [lists, lens, tiles, *blocks] + ([] if acc is None else [acc])
    scratch = [pltpu.VMEM((total, TILE, width), BF16)]
    if last:
        out_shape = jax.ShapeDtypeStruct((ROW_TILES, TILE, width), BF16)
        scratch = [pltpu.VMEM(shape, F32)] + scratch
    else:
        out_shape = jax.ShapeDtypeStruct(shape, F32)
    return pl.pallas_call(
        body,
        out_shape=out_shape,
        in_specs=[SMEM] * 2 + [VMEM] * (len(ins) - 2),
        out_specs=VMEM,
        scratch_shapes=scratch,
        compiler_params=params(16),
        cost_estimate=pl.CostEstimate(
            flops=2 * n * 12 * TILE * TILE * width, bytes_accessed=n * 5 * TILE * TILE * 2, transcendentals=0
        ),
    )(*ins)


def backward_kernel(k, lists, lens, tiles, mine, theirs):
    n = len(SETS[k]) // 2
    width = (mine.shape[0] - 2 * PART) * 2 // ROW_TILES

    def body(list_ref, len_ref, a_ref, mine_ref, their_ref, *refs):
        outs, other, (g_all, acc_ref) = refs[:n], refs[n], refs[n + 1 :]
        half = ROW_TILES // 2
        for i in range(half):
            g_all[i] = mine_ref[i * width : (i + 1) * width, :]
            g_all[half + i] = their_ref[i * width : (i + 1) * width, :]
        g_all[2 * half] = jnp.zeros_like(g_all[2 * half])
        acc_ref[...] = jnp.zeros_like(acc_ref)

        def step(tile, near, place):
            acc_ref[near] += jnp.dot(g_all[place], a_ref[tile], preferred_element_type=F32)

        each_tile(k, list_ref, len_ref, step)
        for i in range(n):
            for t in range(2):
                outs[i][:, t * TILE : (t + 1) * TILE] = acc_ref[4 * i + t].astype(BF16)
                other[i, :, t * TILE : (t + 1) * TILE] = acc_ref[4 * i + 2 + t].astype(BF16)

    result = pl.pallas_call(
        body,
        out_shape=[jax.ShapeDtypeStruct((width, 2 * TILE), BF16)] * n
        + [jax.ShapeDtypeStruct((n, width, 2 * TILE), BF16)],
        in_specs=[SMEM] * 2 + [VMEM] * 3,
        out_specs=[VMEM] * (n + 1),
        scratch_shapes=[
            pltpu.VMEM((ROW_TILES + 1, width, TILE), BF16),
            pltpu.VMEM((4 * n + 1, width, TILE), F32),
        ],
        compiler_params=params(16),
        cost_estimate=pl.CostEstimate(
            flops=4 * n * 12 * TILE * TILE * width, bytes_accessed=n * 10 * TILE * TILE * 2, transcendentals=0
        ),
    )(lists, lens, tiles, mine, theirs)
    return result[:n], result[n]


def join_kernel(pieces):
    sizes = [p.shape[0] for p in pieces]

    def body(*refs):
        at = 0
        for ref, size in zip(refs, sizes):
            refs[-1][at : at + size] = ref[...]
            at += size

    return pl.pallas_call(
        body,
        out_shape=jax.ShapeDtypeStruct((sum(sizes),) + pieces[0].shape[1:], pieces[0].dtype),
        in_specs=[VMEM] * len(pieces),
        out_specs=VMEM,
        compiler_params=params(16),
    )(*pieces)


NT = (((1,), (1,)), ((), ()))
TN = (((0,), (0,)), ((), ()))


PART = 64 + 16


def dense_body(x_ref, parts_ref, cot_ref, ws_ref, wn_ref, bias_ref, out_ref, own_ref, send_ref):
    agg = parts_ref[0].astype(F32)
    for i in range(1, parts_ref.shape[0]):
        agg = agg + parts_ref[i].astype(F32)
    agg = agg.astype(BF16)
    z = (
        jnp.dot(x_ref[...], ws_ref[...], preferred_element_type=F32)
        + jnp.dot(agg, wn_ref[...], preferred_element_type=F32)
        + bias_ref[...]
    )
    sig = jax.nn.sigmoid(z)
    out_ref[...] = (z * sig).astype(BF16)
    dz = (cot_ref[...].astype(F32) * sig * (1.0 + z * (1.0 - sig))).astype(BF16)
    own_ref[...] = lax.dot_general(dz, ws_ref[...], NT, preferred_element_type=F32)
    dagg = lax.dot_general(wn_ref[...], dz, NT, preferred_element_type=F32).astype(BF16)
    grads = [
        lax.dot_general(left, dz, TN, preferred_element_type=F32).astype(BF16) for left in (x_ref[...], agg)
    ]
    total = jnp.sum(dz.astype(F32), axis=0, keepdims=True)
    total = jnp.broadcast_to(total, (16, total.shape[1])).astype(BF16)
    f = dagg.shape[0]
    for d in range(8):
        part = grads[d // 4][(d % 4) * 64 : (d % 4 + 1) * 64]
        for t in range(2):
            half = slice(t * TILE, (t + 1) * TILE)
            send_ref[d, t * f : (t + 1) * f, :] = dagg[:, half]
            send_ref[d, 2 * f + t * 64 : 2 * f + (t + 1) * 64, :] = part[:, half]
            send_ref[d, 2 * f + 128 + t * 16 : 2 * f + 128 + (t + 1) * 16, :] = total[:, half]


def dense_kernel(x, parts, cot, w_self, w_neigh, bias):
    n, f = x.shape
    return pl.pallas_call(
        dense_body,
        out_shape=[
            jax.ShapeDtypeStruct((n, f), BF16),
            jax.ShapeDtypeStruct((n, f), F32),
            jax.ShapeDtypeStruct((8, 2 * f + 2 * PART, TILE), BF16),
        ],
        in_specs=[VMEM] * 6,
        out_specs=[VMEM] * 3,
        compiler_params=params(16),
    )(x, parts, cot, w_self, w_neigh, bias)


def gathered_kernel(received):
    n, rows, lanes = received.shape
    tiles = rows - 2 * PART

    def body(ref, out):
        total = None
        for d in range(n):
            out[d * tiles : (d + 1) * tiles, :] = ref[d, 0:tiles, :]
            part = ref[d, tiles:rows, :].astype(F32)
            total = part if total is None else total + part
        out[n * tiles :, :] = total.astype(BF16)

    return pl.pallas_call(
        body,
        out_shape=jax.ShapeDtypeStruct((n * tiles + 2 * PART, lanes), BF16),
        in_specs=[VMEM],
        out_specs=VMEM,
        compiler_params=params(16),
    )(received)


def rider_kernel(mine, theirs):
    at = mine.shape[0] - 2 * PART

    def body(a_ref, b_ref, out):
        total = (a_ref[at:, :].astype(F32) + b_ref[at:, :].astype(F32)).astype(BF16)
        for t in range(2):
            out[0:64, t * TILE : (t + 1) * TILE] = total[t * 64 : (t + 1) * 64]
            out[64:PART, t * TILE : (t + 1) * TILE] = total[128 + t * 16 : 128 + (t + 1) * 16]

    return pl.pallas_call(
        body,
        out_shape=jax.ShapeDtypeStruct((PART, 2 * TILE), BF16),
        in_specs=[VMEM] * 2,
        out_specs=VMEM,
        compiler_params=params(16),
    )(mine, theirs)


def hop_kernel(terms, moving, w):
    refs = [t[0] if isinstance(t, tuple) else t for t in terms]
    at = [t[1] if isinstance(t, tuple) else None for t in terms]
    width = refs[0].shape[-1]
    rows = width
    ins = refs + [v for v in (moving, w) if v is not None and v is not False]

    def body(*refs):
        out = refs[-1]
        total = None
        for ref, i in zip(refs, at):
            term = (ref[0:rows, :] if i is None else ref[i]).astype(F32)
            total = term if total is None else total + term
        if moving is not None:
            total = total + refs[len(at)][0:rows, :].astype(F32)
        out[0:rows, :] = total.astype(BF16)
        if w is None:
            out[rows:, :] = refs[len(at)][rows:, :]
        elif w is not False:
            out[rows:, :] = refs[-2][...]

    return pl.pallas_call(
        body,
        out_shape=jax.ShapeDtypeStruct((rows + (0 if w is False else PART), width), BF16),
        in_specs=[VMEM] * len(ins),
        out_specs=VMEM,
        compiler_params=params(16),
    )(*ins)


def total_kernel(w, ups, downs):
    n = len(ups) + len(downs) + 1
    rows = ups[0].shape[0] - PART

    def body(*refs):
        out, all_ref = refs[-2:]
        z = axes()[0]
        all_ref[z & 3] = refs[0][...]
        for j in range(len(ups)):
            all_ref[(z - 1 - j) & 3] = refs[1 + j][rows:, :]
        for j in range(len(downs)):
            all_ref[(z + 1 + j) & 3] = refs[1 + len(ups) + j][rows:, :]
        total = all_ref[0].astype(F32)
        for i in range(1, n):
            total = total + all_ref[i].astype(F32)
        out[...] = total.astype(BF16)

    return pl.pallas_call(
        body,
        out_shape=jax.ShapeDtypeStruct(w.shape, BF16),
        in_specs=[VMEM] * n,
        out_specs=VMEM,
        scratch_shapes=[pltpu.VMEM((n,) + w.shape, BF16)],
        compiler_params=params(16),
    )(w, *ups, *downs)


def features_kernel(own, t, up, down, y):
    n, f = own.shape

    def body(own_ref, t_ref, up_ref, down_ref, y_ref, out):
        spread = (
            t_ref[...].astype(F32) + up_ref[0:f, :].astype(F32) + down_ref[0:f, :].astype(F32) + y_ref[...].astype(F32)
        )
        out[...] = (own_ref[...] + spread.T).astype(BF16)

    return pl.pallas_call(
        body,
        out_shape=jax.ShapeDtypeStruct((n, f), BF16),
        in_specs=[VMEM] * 5,
        out_specs=VMEM,
        compiler_params=params(16),
    )(own, t, up, down, y)


def weights_kernel(pairs):
    f = pairs[0].shape[1]

    def body(*refs):
        gs_ref, gn_ref, gb_ref = refs[-3:]
        z, yl, yh, x, core = axes()
        for j in range(NX):
            at = (x + j) & (NX - 1)
            rows = pl.ds(pl.multiple_of(at * 64, 64), 64)
            for h, out in enumerate((gs_ref, gn_ref)):
                start = pl.multiple_of((yh ^ h) * PART, 16)
                out[rows, :] = refs[j][pl.ds(start, 64), :].astype(F32)

            @pl.when(at == 0)
            def _():
                start = pl.multiple_of(yh * PART + 64, 16)
                gb_ref[...] = refs[j][pl.ds(start, 16), :].astype(F32)[0:1]

    sq = jax.ShapeDtypeStruct((f, f), F32)
    return pl.pallas_call(
        body,
        out_shape=[sq, sq, jax.ShapeDtypeStruct((1, f), F32)],
        in_specs=[VMEM] * NX,
        out_specs=[VMEM] * 3,
        compiler_params=params(16),
    )(*pairs)


def add(*terms):
    total = terms[0].astype(F32)
    for t in terms[1:]:
        total = total + t.astype(F32)
    return total.astype(BF16)


def after(value, *done):
    return lax.optimization_barrier((value, *done))[0]


def local(features, w_self, w_neigh, bias, cotangent, tile_values, tile_rows, tile_cols, tile_counts):
    width = features.shape[1]
    lists, lens = list_kernel(tile_rows[0, 0].T, tile_cols[0, 0].T, tile_counts[0, 0])
    tiles = load_kernel(tile_values.reshape((-1,) + tile_values.shape[4:]))

    together = lax.optimization_barrier
    got = {(0, 0): features}
    got[0, 1] = after(permute(features, dyl=1), tiles)
    for k in (1, 2, 3):
        for dy in (0, 1):
            got[-k, dy] = permute(got[1 - k, dy], dz=1)
            got[k, dy] = permute(got[k - 1, dy], dz=-1)
        if k == 1:
            got[1, 0] = after(got[1, 0], lists)
        if k == 2:
            acc = forward_kernel((0,), lists, lens, tiles, got, None, False)
            got[2, 1], acc = together((got[2, 1], acc))
        if k == 3:
            acc = forward_kernel((1,), lists, lens, tiles, got, acc, False)
            got[3, 1], acc = together((got[3, 1], acc))
    got[4, 0] = permute(got[-3, 0], dz=1)
    got[4, 1] = permute(got[3, 1], dz=-1)
    acc = forward_kernel((2,), lists, lens, tiles, got, acc, False)
    partial = forward_kernel((3,), lists, lens, tiles, got, acc, True)

    chips = [[q * NC + c for q in range(NYH * NX)] for c in range(NC)]
    partial = partial.reshape(2, 16 * TILE, width)
    half = add(partial[0], permute(partial[1], dc=1)).reshape(8, 2 * TILE, width)
    parts = lax.all_to_all(half, "rep", 0, 0, axis_index_groups=chips, tiled=True)

    output, own, send = dense_kernel(features, parts, cotangent, w_self, w_neigh, bias.reshape(1, width))

    mine = gathered_kernel(lax.all_to_all(send, "rep", 0, 0, axis_index_groups=chips, tiled=True))
    theirs = permute(mine, dc=1)

    def products(k):
        return backward_kernel(k, lists, lens, tiles, mine, theirs)

    w = rider_kernel(mine, theirs)
    (t4,), u4 = products(3)
    theirs, u4 = together((theirs, u4))
    (t3, t3d), u3 = products(2)
    y4 = permute(u4, dyl=1)
    w = add(w, permute(w, dz=4))
    y4, w, theirs, u3 = together((y4, w, theirs, u3))
    (t2, t2d), u2 = products(1)
    up1, y3, theirs, u2 = together(
        (permute(hop_kernel([t4, (y4, 0)], None, w), dz=1), permute(u3, dyl=1), theirs, u2)
    )
    (t0, t1, t1d), u1 = products(0)
    up2, down1, y2, u1 = together(
        (
            permute(hop_kernel([t3, (y3, 0)], up1, None), dz=1),
            permute(hop_kernel([t3d, (y3, 1)], None, w), dz=-1),
            permute(u2, dyl=1),
            u1,
        )
    )
    w = total_kernel(w, [up1, up2], [down1])
    u1 = u1.reshape(3 * width, -1)
    up3, down2, y1 = together(
        (
            permute(hop_kernel([t2, (y2, 0)], up2, False), dz=1),
            permute(hop_kernel([t2d, (y2, 1)], down1, False), dz=-1),
            permute(join_kernel([u1[width:], w]), dyl=1),
        )
    )
    w = add(w, y1[2 * width :])
    up4, down3, y0, w_y = together(
        (
            permute(hop_kernel([t1, y1], up3, False), dz=1),
            permute(hop_kernel([t1d, (y1, slice(width, 2 * width))], down2, False), dz=-1),
            permute(u1[:width], dyl=1),
            permute(w, dyh=1),
        )
    )
    grad_features = features_kernel(own, t0, up4, down3, y0)
    pair = join_kernel([w, w_y])
    grad_self, grad_neigh, grad_bias = weights_kernel(
        [pair, permute(pair, dx=-1), permute(pair, dx=2), permute(pair, dx=1)]
    )
    return (output, grad_features, grad_self, grad_neigh, grad_bias.reshape(width))


def solution(mesh):
    in_specs = (
        P(("blk", "rep"), None),
        P(),
        P(),
        P(),
        P(("blk", "rep"), None),
        P("blk", "rep", None, None, None, None),
        P("blk", "rep", None, None),
        P("blk", "rep", None, None),
        P("blk", "rep", None),
    )
    out_specs = (P(("blk", "rep"), None), P(("blk", "rep"), None), P(), P(), P())
    return jax.shard_map(local, mesh=mesh, in_specs=in_specs, out_specs=out_specs, check_vma=False)
```

```python
import jax
import jax.numpy as jnp
from jax import lax
from jax.experimental import pallas as pl
from jax.experimental.pallas import tpu as pltpu
from jax.sharding import PartitionSpec as P

F32 = jnp.float32
BF16 = jnp.bfloat16
NZ, NYL, NYH, NX, NC = 8, 2, 2, 4, 2
TILE = 128
SMEM = pl.BlockSpec(memory_space=pltpu.SMEM)
VMEM = pl.BlockSpec(memory_space=pltpu.VMEM)
MB = 1024 * 1024


def permute(value, dz=0, dyl=0, dyh=0, dx=0, dc=0):
    pairs = []
    for z in range(NZ):
        to_z = (z + (dz(z) if callable(dz) else dz)) % NZ
        for yl in range(NYL):
            for yh in range(NYH):
                for x in range(NX):
                    to_x = (x + (dx(x) if callable(dx) else dx)) % NX
                    for c in range(NC):
                        src = (((z * NYL + yl) * NYH + yh) * NX + x) * NC + c
                        dst = (((to_z * NYL + (yl + dyl) % NYL) * NYH + (yh + dyh) % NYH) * NX + to_x) * NC
                        pairs.append((src, dst + (c + dc) % NC))
    return lax.ppermute(value, ("blk", "rep"), pairs)


def params(mib):
    return pltpu.CompilerParams(vmem_limit_bytes=mib * MB)


def axes():
    b, r = lax.axis_index("blk"), lax.axis_index("rep")
    return b >> 1, b & 1, r >> 3, (r >> 1) & 3, r & 1


SETS = (
    ((0, 0), (0, 1), (1, 0), (1, 1), (-1, 0), (-1, 1)),
    ((2, 0), (2, 1), (-2, 0), (-2, 1)),
    ((3, 0), (3, 1), (-3, 0), (-3, 1)),
    ((4, 0), (4, 1)),
)
UNROLL = 16
LIST = 6 * 12 + UNROLL
ROW_TILES = 32


def list_body(rows_ref, cols_ref, cnt_ref, list_ref, len_ref):
    z, yl, yh, x, core = axes()
    slots = rows_ref.shape[0]
    for k, offsets in enumerate(SETS):
        n = jnp.int32(0)
        for i, (dz, dy) in enumerate(offsets):
            c = ((z + dz + NZ) & (NZ - 1)) * 2 + (yl ^ dy)

            def put(s, _, c=c, i=i, k=k, n=n):
                row = rows_ref[s, c]
                q = row >> 1
                place = ((q & 1) ^ core) * 16 + (q >> 1) * 2 + (row & 1)
                near = i * 2 + cols_ref[s, c]
                list_ref[k, n + s] = (c * slots + s) | (near << 8) | (place << 16)
                return 0

            lax.fori_loop(0, cnt_ref[c], put, 0)
            n = n + cnt_ref[c]
        len_ref[k] = (n + UNROLL - 1) // UNROLL
        for s in range(UNROLL):
            list_ref[k, n + s] = ((2 * len(offsets)) << 8) | (ROW_TILES << 16)


def list_kernel(rows, cols, counts):
    return pl.pallas_call(
        list_body,
        out_shape=[
            jax.ShapeDtypeStruct((len(SETS), LIST), jnp.int32),
            jax.ShapeDtypeStruct((len(SETS),), jnp.int32),
        ],
        in_specs=[SMEM] * 3,
        out_specs=[SMEM] * 2,
        compiler_params=params(16),
    )(rows, cols, counts)


def load_kernel(values):
    def body(hbm, out, sem):
        copy = pltpu.make_async_copy(hbm, out, sem)
        copy.start()
        copy.wait()

    return pl.pallas_call(
        body,
        out_shape=jax.ShapeDtypeStruct(values.shape, values.dtype),
        in_specs=[pl.BlockSpec(memory_space=pltpu.HBM)],
        out_specs=VMEM,
        scratch_shapes=[pltpu.SemaphoreType.DMA],
        compiler_params=params(16),
    )(values)


def each_tile(k, list_ref, len_ref, step):
    def some(j, _):
        for u in range(UNROLL):
            e = list_ref[k, j * UNROLL + u]
            step(e & 255, (e >> 8) & 255, e >> 16)
        return 0

    lax.fori_loop(0, len_ref[k], some, 0)


def bases(sets):
    at, out = 0, []
    for k in sets:
        out.append(at)
        at += 2 * len(SETS[k]) + 1
    return out, at


def forward_kernel(sets, lists, lens, tiles, got, acc, last):
    blocks = [got[o] for k in sets for o in SETS[k]]
    n = len(blocks)
    width = blocks[0].shape[1]
    shape = (ROW_TILES + 1, TILE, width)
    starts, total = bases(sets)

    def body(list_ref, len_ref, a_ref, *refs):
        x_refs, rest = refs[:n], refs[n:]
        x_all = rest[-1]
        acc_ref = rest[-2]
        if acc is None:
            acc_ref[...] = jnp.zeros_like(acc_ref)
        else:
            acc_ref[...] = rest[0][...]
        x_iter = iter(x_refs)
        for k, start in zip(sets, starts):
            for i in range(len(SETS[k])):
                ref = next(x_iter)
                for t in range(2):
                    x_all[start + 2 * i + t] = ref[t * TILE : (t + 1) * TILE, :]
            x_all[start + 2 * len(SETS[k])] = jnp.zeros_like(x_all[0])
        for k, start in zip(sets, starts):

            def step(tile, near, place, start=start):
                acc_ref[place] += jnp.dot(a_ref[tile], x_all[start + near], preferred_element_type=F32)

            each_tile(k, list_ref, len_ref, step)
        if last:
            out_ref = rest[-3]
            for p in range(ROW_TILES):
                out_ref[p] = acc_ref[p].astype(BF16)

    ins = [lists, lens, tiles, *blocks] + ([] if acc is None else [acc])
    scratch = [pltpu.VMEM((total, TILE, width), BF16)]
    if last:
        out_shape = jax.ShapeDtypeStruct((ROW_TILES, TILE, width), BF16)
        scratch = [pltpu.VMEM(shape, F32)] + scratch
    else:
        out_shape = jax.ShapeDtypeStruct(shape, F32)
    return pl.pallas_call(
        body,
        out_shape=out_shape,
        in_specs=[SMEM] * 2 + [VMEM] * (len(ins) - 2),
        out_specs=VMEM,
        scratch_shapes=scratch,
        compiler_params=params(16),
        cost_estimate=pl.CostEstimate(
            flops=2 * n * 12 * TILE * TILE * width, bytes_accessed=n * 5 * TILE * TILE * 2, transcendentals=0
        ),
    )(*ins)


def backward_kernel(k, lists, lens, tiles, mine, theirs):
    n = len(SETS[k]) // 2
    width = (mine.shape[0] - 2 * PART) * 2 // ROW_TILES

    def body(list_ref, len_ref, a_ref, mine_ref, their_ref, *refs):
        outs, other, (g_all, acc_ref) = refs[:n], refs[n], refs[n + 1 :]
        half = ROW_TILES // 2
        for i in range(half):
            g_all[i] = mine_ref[i * width : (i + 1) * width, :]
            g_all[half + i] = their_ref[i * width : (i + 1) * width, :]
        g_all[2 * half] = jnp.zeros_like(g_all[2 * half])
        acc_ref[...] = jnp.zeros_like(acc_ref)

        def step(tile, near, place):
            acc_ref[near] += jnp.dot(g_all[place], a_ref[tile], preferred_element_type=F32)

        each_tile(k, list_ref, len_ref, step)
        for i in range(n):
            for t in range(2):
                outs[i][:, t * TILE : (t + 1) * TILE] = acc_ref[4 * i + t].astype(BF16)
                other[i, :, t * TILE : (t + 1) * TILE] = acc_ref[4 * i + 2 + t].astype(BF16)

    result = pl.pallas_call(
        body,
        out_shape=[jax.ShapeDtypeStruct((width, 2 * TILE), BF16)] * n
        + [jax.ShapeDtypeStruct((n, width, 2 * TILE), BF16)],
        in_specs=[SMEM] * 2 + [VMEM] * 3,
        out_specs=[VMEM] * (n + 1),
        scratch_shapes=[
            pltpu.VMEM((ROW_TILES + 1, width, TILE), BF16),
            pltpu.VMEM((4 * n + 1, width, TILE), F32),
        ],
        compiler_params=params(16),
        cost_estimate=pl.CostEstimate(
            flops=4 * n * 12 * TILE * TILE * width, bytes_accessed=n * 10 * TILE * TILE * 2, transcendentals=0
        ),
    )(lists, lens, tiles, mine, theirs)
    return result[:n], result[n]


def join_kernel(pieces):
    sizes = [p.shape[0] for p in pieces]

    def body(*refs):
        at = 0
        for ref, size in zip(refs, sizes):
            refs[-1][at : at + size] = ref[...]
            at += size

    return pl.pallas_call(
        body,
        out_shape=jax.ShapeDtypeStruct((sum(sizes),) + pieces[0].shape[1:], pieces[0].dtype),
        in_specs=[VMEM] * len(pieces),
        out_specs=VMEM,
        compiler_params=params(16),
    )(*pieces)


NT = (((1,), (1,)), ((), ()))
TN = (((0,), (0,)), ((), ()))


PART = 64 + 16


def dense_body(x_ref, parts_ref, cot_ref, ws_ref, wn_ref, bias_ref, out_ref, own_ref, send_ref):
    agg = parts_ref[0].astype(F32)
    for i in range(1, parts_ref.shape[0]):
        agg = agg + parts_ref[i].astype(F32)
    agg = agg.astype(BF16)
    z = (
        jnp.dot(x_ref[...], ws_ref[...], preferred_element_type=F32)
        + jnp.dot(agg, wn_ref[...], preferred_element_type=F32)
        + bias_ref[...]
    )
    sig = jax.nn.sigmoid(z)
    out_ref[...] = (z * sig).astype(BF16)
    dz = (cot_ref[...].astype(F32) * sig * (1.0 + z * (1.0 - sig))).astype(BF16)
    own_ref[...] = lax.dot_general(dz, ws_ref[...], NT, preferred_element_type=F32)
    dagg = lax.dot_general(wn_ref[...], dz, NT, preferred_element_type=F32).astype(BF16)
    grads = [
        lax.dot_general(left, dz, TN, preferred_element_type=F32).astype(BF16) for left in (x_ref[...], agg)
    ]
    total = jnp.sum(dz.astype(F32), axis=0, keepdims=True)
    total = jnp.broadcast_to(total, (16, total.shape[1])).astype(BF16)
    f = dagg.shape[0]
    for d in range(8):
        part = grads[d // 4][(d % 4) * 64 : (d % 4 + 1) * 64]
        for t in range(2):
            half = slice(t * TILE, (t + 1) * TILE)
            send_ref[d, t * f : (t + 1) * f, :] = dagg[:, half]
            send_ref[d, 2 * f + t * 64 : 2 * f + (t + 1) * 64, :] = part[:, half]
            send_ref[d, 2 * f + 128 + t * 16 : 2 * f + 128 + (t + 1) * 16, :] = total[:, half]


def dense_kernel(x, parts, cot, w_self, w_neigh, bias):
    n, f = x.shape
    return pl.pallas_call(
        dense_body,
        out_shape=[
            jax.ShapeDtypeStruct((n, f), BF16),
            jax.ShapeDtypeStruct((n, f), F32),
            jax.ShapeDtypeStruct((8, 2 * f + 2 * PART, TILE), BF16),
        ],
        in_specs=[VMEM] * 6,
        out_specs=[VMEM] * 3,
        compiler_params=params(16),
    )(x, parts, cot, w_self, w_neigh, bias)


def gathered_kernel(received):
    n, rows, lanes = received.shape
    tiles = rows - 2 * PART

    def body(ref, out):
        total = None
        for d in range(n):
            out[d * tiles : (d + 1) * tiles, :] = ref[d, 0:tiles, :]
            part = ref[d, tiles:rows, :].astype(F32)
            total = part if total is None else total + part
        out[n * tiles :, :] = total.astype(BF16)

    return pl.pallas_call(
        body,
        out_shape=jax.ShapeDtypeStruct((n * tiles + 2 * PART, lanes), BF16),
        in_specs=[VMEM],
        out_specs=VMEM,
        compiler_params=params(16),
    )(received)


def rider_kernel(mine, theirs):
    at = mine.shape[0] - 2 * PART

    def body(a_ref, b_ref, out):
        total = (a_ref[at:, :].astype(F32) + b_ref[at:, :].astype(F32)).astype(BF16)
        for t in range(2):
            out[0:64, t * TILE : (t + 1) * TILE] = total[t * 64 : (t + 1) * 64]
            out[64:PART, t * TILE : (t + 1) * TILE] = total[128 + t * 16 : 128 + (t + 1) * 16]

    return pl.pallas_call(
        body,
        out_shape=jax.ShapeDtypeStruct((PART, 2 * TILE), BF16),
        in_specs=[VMEM] * 2,
        out_specs=VMEM,
        compiler_params=params(16),
    )(mine, theirs)


def hop_kernel(terms, moving, w):
    refs = [t[0] if isinstance(t, tuple) else t for t in terms]
    at = [t[1] if isinstance(t, tuple) else None for t in terms]
    width = refs[0].shape[-1]
    rows = width
    ins = refs + [v for v in (moving, w) if v is not None and v is not False]

    def body(*refs):
        out = refs[-1]
        total = None
        for ref, i in zip(refs, at):
            term = (ref[0:rows, :] if i is None else ref[i]).astype(F32)
            total = term if total is None else total + term
        if moving is not None:
            total = total + refs[len(at)][0:rows, :].astype(F32)
        out[0:rows, :] = total.astype(BF16)
        if w is None:
            out[rows:, :] = refs[len(at)][rows:, :]
        elif w is not False:
            out[rows:, :] = refs[-2][...]

    return pl.pallas_call(
        body,
        out_shape=jax.ShapeDtypeStruct((rows + (0 if w is False else PART), width), BF16),
        in_specs=[VMEM] * len(ins),
        out_specs=VMEM,
        compiler_params=params(16),
    )(*ins)


def total_kernel(w, ups, downs):
    n = len(ups) + len(downs) + 1
    rows = ups[0].shape[0] - PART

    def body(*refs):
        out, all_ref = refs[-2:]
        z = axes()[0]
        all_ref[z & 3] = refs[0][...]
        for j in range(len(ups)):
            all_ref[(z - 1 - j) & 3] = refs[1 + j][rows:, :]
        for j in range(len(downs)):
            all_ref[(z + 1 + j) & 3] = refs[1 + len(ups) + j][rows:, :]
        total = all_ref[0].astype(F32)
        for i in range(1, n):
            total = total + all_ref[i].astype(F32)
        out[...] = total.astype(BF16)

    return pl.pallas_call(
        body,
        out_shape=jax.ShapeDtypeStruct(w.shape, BF16),
        in_specs=[VMEM] * n,
        out_specs=VMEM,
        scratch_shapes=[pltpu.VMEM((n,) + w.shape, BF16)],
        compiler_params=params(16),
    )(w, *ups, *downs)


def features_kernel(own, t, up, down, y):
    n, f = own.shape

    def body(own_ref, t_ref, up_ref, down_ref, y_ref, out):
        spread = (
            t_ref[...].astype(F32) + up_ref[0:f, :].astype(F32) + down_ref[0:f, :].astype(F32) + y_ref[...].astype(F32)
        )
        out[...] = (own_ref[...] + spread.T).astype(BF16)

    return pl.pallas_call(
        body,
        out_shape=jax.ShapeDtypeStruct((n, f), BF16),
        in_specs=[VMEM] * 5,
        out_specs=VMEM,
        compiler_params=params(16),
    )(own, t, up, down, y)


def weights_kernel(parts):
    n, rows, f = parts.shape

    def body(ref, gs_ref, gn_ref, gb_ref):
        for d in range(n):
            out = gs_ref if d < n // 2 else gn_ref
            at = d % (n // 2) * 64
            out[at : at + 64, :] = ref[d, 0:64, :].astype(F32)
        gb_ref[...] = ref[0, 64:PART, :].astype(F32)[0:1]

    sq = jax.ShapeDtypeStruct((f, f), F32)
    return pl.pallas_call(
        body,
        out_shape=[sq, sq, jax.ShapeDtypeStruct((1, f), F32)],
        in_specs=[VMEM],
        out_specs=[VMEM] * 3,
        compiler_params=params(16),
    )(parts)


def add(*terms):
    total = terms[0].astype(F32)
    for t in terms[1:]:
        total = total + t.astype(F32)
    return total.astype(BF16)


def after(value, *done):
    return lax.optimization_barrier((value, *done))[0]


def local(features, w_self, w_neigh, bias, cotangent, tile_values, tile_rows, tile_cols, tile_counts):
    width = features.shape[1]
    lists, lens = list_kernel(tile_rows[0, 0].T, tile_cols[0, 0].T, tile_counts[0, 0])
    tiles = load_kernel(tile_values.reshape((-1,) + tile_values.shape[4:]))

    together = lax.optimization_barrier
    got = {(0, 0): features}
    got[0, 1] = after(permute(features, dyl=1), tiles)
    for k in (1, 2, 3):
        for dy in (0, 1):
            got[-k, dy] = permute(got[1 - k, dy], dz=1)
            got[k, dy] = permute(got[k - 1, dy], dz=-1)
        if k == 1:
            got[1, 0] = after(got[1, 0], lists)
        if k == 2:
            acc = forward_kernel((0,), lists, lens, tiles, got, None, False)
            got[2, 1], acc = together((got[2, 1], acc))
        if k == 3:
            acc = forward_kernel((1,), lists, lens, tiles, got, acc, False)
            got[3, 1], acc = together((got[3, 1], acc))
    got[4, 0] = permute(got[-3, 0], dz=1)
    got[4, 1] = permute(got[3, 1], dz=-1)
    acc = forward_kernel((2,), lists, lens, tiles, got, acc, False)
    partial = forward_kernel((3,), lists, lens, tiles, got, acc, True)

    chips = [[q * NC + c for q in range(NYH * NX)] for c in range(NC)]
    partial = partial.reshape(2, 16 * TILE, width)
    half = add(partial[0], permute(partial[1], dc=1)).reshape(8, 2 * TILE, width)
    parts = lax.all_to_all(half, "rep", 0, 0, axis_index_groups=chips, tiled=True)

    output, own, send = dense_kernel(features, parts, cotangent, w_self, w_neigh, bias.reshape(1, width))

    mine = gathered_kernel(lax.all_to_all(send, "rep", 0, 0, axis_index_groups=chips, tiled=True))
    theirs = permute(mine, dc=1)

    def products(k):
        return backward_kernel(k, lists, lens, tiles, mine, theirs)

    w = rider_kernel(mine, theirs)
    (t4,), u4 = products(3)
    theirs, u4 = together((theirs, u4))
    (t3, t3d), u3 = products(2)
    y4 = permute(u4, dyl=1)
    w = add(w, permute(w, dz=4))
    y4, w, theirs, u3 = together((y4, w, theirs, u3))
    (t2, t2d), u2 = products(1)
    up1, y3, theirs, u2 = together(
        (permute(hop_kernel([t4, (y4, 0)], None, w), dz=1), permute(u3, dyl=1), theirs, u2)
    )
    (t0, t1, t1d), u1 = products(0)
    up2, down1, y2, u1 = together(
        (
            permute(hop_kernel([t3, (y3, 0)], up1, None), dz=1),
            permute(hop_kernel([t3d, (y3, 1)], None, w), dz=-1),
            permute(u2, dyl=1),
            u1,
        )
    )
    w = total_kernel(w, [up1, up2], [down1])
    u1 = u1.reshape(3 * width, -1)
    up3, down2, y1 = together(
        (
            permute(hop_kernel([t2, (y2, 0)], up2, False), dz=1),
            permute(hop_kernel([t2d, (y2, 1)], down1, False), dz=-1),
            permute(join_kernel([u1[width:], w]), dyl=1),
        )
    )
    w = add(w, y1[2 * width :])
    up4 = permute(hop_kernel([t1, y1], up3, False), dz=1)
    down3 = permute(hop_kernel([t1d, (y1, slice(width, 2 * width))], down2, False), dz=-1)
    y0 = permute(u1[:width], dyl=1)
    parts = jnp.broadcast_to(w[None], (len(chips[0]),) + w.shape)
    parts = lax.all_to_all(parts, "rep", 0, 0, axis_index_groups=chips, tiled=True)
    up4, down3, y0, parts = together((up4, down3, y0, parts))
    grad_features = features_kernel(own, t0, up4, down3, y0)
    grad_self, grad_neigh, grad_bias = weights_kernel(parts)
    return (output, grad_features, grad_self, grad_neigh, grad_bias.reshape(width))


def solution(mesh):
    in_specs = (
        P(("blk", "rep"), None),
        P(),
        P(),
        P(),
        P(("blk", "rep"), None),
        P("blk", "rep", None, None, None, None),
        P("blk", "rep", None, None),
        P("blk", "rep", None, None),
        P("blk", "rep", None),
    )
    out_specs = (P(("blk", "rep"), None), P(("blk", "rep"), None), P(), P(), P())
    return jax.shard_map(local, mesh=mesh, in_specs=in_specs, out_specs=out_specs, check_vma=False)
```
